32 devices in a mesh: dp: 16 (over z, y, core), tile: 2 (over x).
Axes of the slice: x: 2, y: 2, z: 4, core: 2. Of those that a mesh axis runs over, the one named last changes fastest.
Arguments:
- frames: bfloat16 [16, 2, 3, 32, 128], P('dp', None, None, 'tile'), may hold values from 0 to 1
- features: bfloat16 [16, 64, 32, 128], P('dp', None, 'tile'), may hold values from -6 to 6
- cotangent: float32 [16, 3, 32, 128], P('dp', None, 'tile'), may hold values from -6 to 6
- head_weight: bfloat16 [108, 576], replicated, may hold values from -0.25 to 0.25
Outputs:
- grad_weight: float32 [108, 576], replicated
- grad_features: float32 [16, 64, 32, 128], P('dp', None, 'tile')
- grad_frames: float32 [16, 2, 3, 32, 128], P('dp', None, None, 'tile')
The draws below stay inside these ranges and needn't reach their ends.
All inputs are finite; a program needn't handle non-finite values.
Results may differ from the reference program's by a relative error of at most 0.003.
Values may be sent and summed in bfloat16 or wider, within the bound.
A program may use at most 64 MiB of HBM per device.

```python
import jax
import jax.numpy as jnp
from jax import lax

C = 64
W = 128
KOUT = 108
H = 32
PAIRS = 16


def spiked(entries, own_key, source, target, blocks, factor):
    def block_of(dim):
        return (jnp.arange(entries.shape[dim]) // (entries.shape[dim] // blocks)).reshape((-1,) + (1,) * (entries.ndim - 1 - dim))

    near = jax.random.permutation(own_key, blocks)[block_of(target)]
    second = (block_of(target) + blocks // 2) % blocks
    return jnp.where((block_of(source) == near) | (block_of(source) == second), factor * entries, entries)


def shard_levels(rng, extent, pieces, smallest, largest):
    factor_of, own = 1.0, jax.random.fold_in(rng, 6)
    for dim, shards_of in pieces:
        heights = jnp.exp(jax.random.uniform(jax.random.fold_in(own, dim), (shards_of,), jnp.float32, smallest / len(pieces), largest / len(pieces)))
        factor_of = factor_of * jnp.repeat(heights, extent[dim] // shards_of).reshape([-1 if axis == dim else 1 for axis in range(len(extent))])
    return factor_of


def normal_values(rng, dims, scale, limit, split=(), held_as=jnp.bfloat16):
    loudness = shard_levels(rng, dims, split, -0.22, 0.18) if split else 1.0
    result = jax.random.normal(rng, dims, jnp.float32) * scale * loudness
    return jnp.minimum(jnp.maximum(result, -limit), limit).astype(held_as)


def noise_with(key, dims, deviation, limit, shards, heavy, kind=jnp.bfloat16):
    result = deviation * jax.random.normal(key, dims, jnp.float32)
    if shards:
        result = result * shard_levels(key, dims, shards, -0.22, 0.18)
    return jnp.clip(spiked(result, jax.random.fold_in(key, 3), *heavy), -limit, limit).astype(kind)


def setup_inputs(seed: int = 0) -> dict:
    key_list = jax.random.split(jax.random.key(seed), 5)
    return {
        "frames": jnp.clip(1.0 * jax.random.uniform(key_list[0], (PAIRS, 2, 3, H, W), jnp.float32) ** shard_levels(key_list[0], (PAIRS, 2, 3, H, W), ((0, 16), (3, 2)), -0.2, 0.2), 0.0, 1.0).astype(jnp.bfloat16),
        "features": noise_with(key_list[1], (PAIRS, C, H, W), 1.0, 6.0, ((0, 16), (2, 2)), (0, 1, 16, 2.0)),
        "cotangent": normal_values(key_list[2], (PAIRS, 3, H, W), 1.0, 6.0, ((0, 16), (2, 2)), jnp.float32),
        "head_weight": normal_values(key_list[3], (KOUT, 9 * C), (9 * C) ** -0.5, 0.25),
    }


def make_patches(padded_map, row_count, col_count):
    blocks = []
    for row_shift in range(3):
        for col_shift in range(3):
            piece = padded_map[:, row_shift:row_shift + row_count, col_shift:col_shift + col_count]
            blocks.append(piece.reshape(piece.shape[0], row_count * col_count))
    return jnp.concatenate(blocks, 0)


def fold_patches(patch_grad, channels, row_count, col_count):
    folded = jnp.zeros((channels, row_count + 2, col_count + 2), jnp.float32)
    slot_index = 0
    for row_shift in range(3):
        for col_shift in range(3):
            block = patch_grad[slot_index * channels:(slot_index + 1) * channels].reshape(channels, row_count, col_count)
            folded = folded.at[:, row_shift:row_shift + row_count, col_shift:col_shift + col_count].add(block)
            slot_index += 1
    return folded


def separable_grads(padded, vertical, horizontal, upstream, group_size):
    tap_count = vertical.shape[0]
    row_count = upstream.shape[1]
    col_count = upstream.shape[2]
    highest = lax.Precision.HIGHEST

    def one_tap(tap_index, carried):
        grad_vert, grad_horiz, grad_padded = carried
        tap_band = lax.dynamic_slice_in_dim(padded, tap_index, row_count, 1)
        window = jnp.stack([tap_band[:, :, col_tap:col_tap + col_count] for col_tap in range(tap_count)])
        blended = jnp.einsum('jyx,jcyx->cyx', horizontal, window, precision=highest)
        grad_vert = lax.dynamic_update_slice_in_dim(grad_vert, jnp.sum(upstream * blended, 0)[None], tap_index, 0)
        scaled = lax.dynamic_index_in_dim(vertical, tap_index, 0, keepdims=False)[None] * upstream
        grad_horiz = grad_horiz + jnp.einsum('cyx,jcyx->jyx', scaled, window, precision=highest)
        spread = horizontal[:, None] * scaled[None]
        back_sum = jnp.zeros((3, row_count, col_count + tap_count - 1), jnp.float32)
        for col_tap in range(tap_count):
            back_sum = back_sum.at[:, :, col_tap:col_tap + col_count].add(spread[col_tap])
        old_rows = lax.dynamic_slice_in_dim(grad_padded, tap_index, row_count, 1)
        grad_padded = lax.dynamic_update_slice_in_dim(grad_padded, old_rows + back_sum, tap_index, 1)
        return grad_vert, grad_horiz, grad_padded

    def group_step(group_index, carried):
        for offset in range(group_size):
            carried = one_tap(group_index * group_size + offset, carried)
        return carried

    start_state = (jnp.zeros(vertical.shape, jnp.float32), jnp.zeros(vertical.shape, jnp.float32),
                   jnp.zeros(padded.shape, jnp.float32))
    return lax.fori_loop(0, tap_count // group_size, group_step, start_state)


def reference(frames, features, cotangent, head_weight):
    tap_count = head_weight.shape[0] // 4
    rim_rows = (tap_count - 1) // 2
    kernel_scale = tap_count ** -0.5

    def one_pair(pair_items):
        pair_frames, feature_map, upstream = pair_items
        channels, row_count, col_count = feature_map.shape
        patches = make_patches(jnp.pad(feature_map, ((0, 0), (1, 1), (1, 1))), row_count, col_count)
        kernels = jnp.dot(head_weight, patches, preferred_element_type=jnp.float32).reshape(-1, row_count, col_count)
        grad_list = []
        frame_list = []
        for which_frame in range(2):
            vertical = kernels[2 * which_frame * tap_count:(2 * which_frame + 1) * tap_count] * kernel_scale
            horizontal = kernels[(2 * which_frame + 1) * tap_count:(2 * which_frame + 2) * tap_count] * kernel_scale
            padded = jnp.pad(pair_frames[which_frame].astype(jnp.float32), ((0, 0), (rim_rows, rim_rows), (rim_rows, rim_rows)))
            grad_vert, grad_horiz, grad_padded = separable_grads(padded, vertical, horizontal, upstream, 1)
            grad_list += [grad_vert, grad_horiz]
            frame_list.append(grad_padded[:, rim_rows:rim_rows + row_count, rim_rows:rim_rows + col_count])
        kernel_grad = (jnp.concatenate(grad_list, 0) * kernel_scale).astype(jnp.bfloat16)
        flat_grad = kernel_grad.reshape(kernel_grad.shape[0], row_count * col_count)
        weight_part = lax.dot_general(flat_grad, patches, (((1,), (1,)), ((), ())), preferred_element_type=jnp.float32)
        patch_grad = lax.dot_general(head_weight, flat_grad, (((0,), (0,)), ((), ())), preferred_element_type=jnp.float32)
        feat_grad = fold_patches(patch_grad, channels, row_count, col_count)[:, 1:row_count + 1, 1:col_count + 1]
        return weight_part, feat_grad, jnp.stack(frame_list)

    pair_parts, feat_grads, frame_grads = lax.map(one_pair, (frames, features, cotangent))
    pixel_count = frames.shape[0] * frames.shape[3] * frames.shape[4]
    weight_sum = jnp.sum(pair_parts, 0) * (pixel_count ** -0.5)
    return weight_sum, feat_grads, frame_grads
```

```python
import functools

import jax
import jax.numpy as jnp
from jax import lax
from jax.experimental import pallas as pl
from jax.experimental.pallas import tpu as pltpu
from jax.sharding import PartitionSpec as P

F32 = jnp.float32
BF16 = jnp.bfloat16
NN = (((1,), (0,)), ((), ()))
NT = (((1,), (1,)), ((), ()))
TN = (((0,), (0,)), ((), ()))


def mm(lhs, rhs, dims):
    return lax.dot_general(lhs, rhs, dims, preferred_element_type=F32)


def halves(value):
    high = value.astype(BF16)
    return high, (value - high.astype(F32)).astype(BF16)


def forward_front(tap_count):
    return -((tap_count - 1) // 2) % 8


def mirror_front(tap_count, cols):
    return (cols - 1 - (tap_count - 1) // 2) % 8


def skew(value, shift):
    count, cols = value.shape
    return jnp.concatenate(
        [
            pltpu.roll(value[row : row + 8], (shift + row) % cols, 1, stride=1, stride_axis=0)
            for row in range(0, count, 8)
        ],
        0,
    )


def local_kernel(
    tap_count,
    feat_ref,
    frame_ref,
    g_ref,
    w_ref,
    wt_ref,
    weight_ref,
    fgrad_ref,
    frim_ref,
    image_ref,
    patch_s,
    kern_s,
    kgrad_s,
    mirror_s,
):
    _, rows, cols = g_ref.shape
    channels = feat_ref.shape[0]
    padded_taps = w_ref.shape[0] // 4
    depth = 3 * channels
    rim = (tap_count - 1) // 2
    scale = tap_count ** (-0.5)
    lane = lax.broadcasted_iota(jnp.int32, (channels, cols), 1)
    first, last = lane == 0, lane == cols - 1

    for row in range(rows + 2):
        at = pl.ds(row * cols, cols)
        piece = feat_ref[:, at]
        wide = piece.astype(F32)
        patch_s[0:channels, at] = jnp.where(first, 0.0, pltpu.roll(wide, 1, 1)).astype(BF16)
        patch_s[channels : 2 * channels, at] = piece
        patch_s[2 * channels : depth, at] = jnp.where(
            last, 0.0, pltpu.roll(wide, cols - 1, 1)
        ).astype(BF16)

    group = 2
    for start in range(0, rows, group):
        stack = jnp.concatenate(
            [patch_s[:, (start + a) * cols : (start + a + group) * cols] for a in range(3)], 0
        )
        kern_s[:, start * cols : (start + group) * cols] = mm(w_ref[...], stack, NN) * scale

    image_ref[...] = jnp.zeros_like(image_ref)
    x_at = lax.broadcasted_iota(jnp.int32, (cols, cols), 0)
    q_at = lax.broadcasted_iota(jnp.int32, (cols, cols), 1)
    band = jnp.abs(q_at - x_at) <= rim
    mirror_band = jnp.abs(cols - 1 - q_at - x_at) <= rim
    in_second = q_at >= 2 * padded_taps
    front = forward_front(tap_count)
    back_shift = mirror_front(tap_count, cols) - (cols + rim - tap_count)

    mirror = jnp.where(q_at + x_at == cols - 1, 1.0, 0.0).astype(BF16)
    for f in range(2):
        for c in range(3):
            mirror_s[f, c] = mm(frame_ref[f, c].astype(BF16), mirror, NN)

    for y in range(rows):
        at = pl.ds(y * cols, cols)
        kern = kern_s[:, at]
        kern_t = jnp.transpose(kern)
        g_rows = [g_ref[c, y : y + 1, :] for c in range(3)]
        vert_parts, horiz_parts = [], []
        for f in range(2):
            base = (2 * f + 1) * padded_taps
            skewed = jnp.where(band, skew(kern_t, -(base + front + rim)), 0.0)
            k_high, k_low = halves(skewed)
            window, mirrored = [
                jnp.concatenate(
                    [ref[f, c, y : y + padded_taps, :] for c in range(3)], 0
                ).astype(BF16)
                for ref in (frame_ref, mirror_s)
            ]
            blend = mm(
                jnp.concatenate([window, window], 1), jnp.concatenate([k_high, k_low], 1), NT
            )
            grad_vert = g_rows[0] * blend[0:padded_taps]
            for c in range(1, 3):
                grad_vert += g_rows[c] * blend[c * padded_taps : (c + 1) * padded_taps]
            vert_parts.append(grad_vert)
            vertical = kern[2 * f * padded_taps : (2 * f + 1) * padded_taps]
            vg_high, vg_low = halves(jnp.concatenate([vertical * g for g in g_rows], 0))
            back = mm(
                jnp.concatenate([vg_high, vg_high], 1), jnp.concatenate([k_high, k_low], 0), NN
            )
            for c in range(3):
                image_ref[f, c, y : y + padded_taps, :] += back[
                    c * padded_taps : (c + 1) * padded_taps
                ]
            cross = mm(
                jnp.concatenate([vg_high, vg_low], 0), jnp.concatenate([mirrored, mirrored], 0), TN
            )
            horiz_parts.append(skew(jnp.where(mirror_band, cross, 0.0), base + back_shift))
        horiz = jnp.transpose(jnp.where(in_second, horiz_parts[1], horiz_parts[0]))
        kgrad_s[:, at] = (
            jnp.concatenate(
                [
                    vert_parts[0],
                    horiz[padded_taps : 2 * padded_taps],
                    vert_parts[1],
                    horiz[3 * padded_taps : 4 * padded_taps],
                ],
                0,
            )
            * scale
        ).astype(BF16)

    for a in range(3):
        part = mm(kgrad_s[...], patch_s[:, a * cols : (a + rows) * cols], NT)
        weight_ref[a] = part

    for row in range(rows + 2):
        total = None
        for a in range(3):
            y = row - a
            if 0 <= y < rows:
                term = mm(
                    wt_ref[a * depth : (a + 1) * depth, :], kgrad_s[:, y * cols : (y + 1) * cols], NN
                )
                total = term if total is None else total + term
        left = total[0:channels]
        right = total[2 * channels : depth]
        result = (
            jnp.where(last, 0.0, pltpu.roll(left, cols - 1, 1))
            + total[channels : 2 * channels]
            + jnp.where(first, 0.0, pltpu.roll(right, 1, 1))
        )
        if row == 0:
            frim_ref[0] = result
        elif row == rows + 1:
            frim_ref[1] = result
        else:
            fgrad_ref[:, row - 1, :] = result


def local_grads(feature_flat, frame_wide, upstream, padded_weight, mirror_weight, tap_count):
    _, rows, cols = upstream.shape
    channels = feature_flat.shape[0]
    outs = padded_weight.shape[0]
    vmem = pl.BlockSpec(memory_space=pltpu.VMEM)
    return pl.pallas_call(
        functools.partial(local_kernel, tap_count),
        out_shape=[
            jax.ShapeDtypeStruct((3, outs, 3 * channels), F32),
            jax.ShapeDtypeStruct((channels, rows, cols), F32),
            jax.ShapeDtypeStruct((2, channels, cols), F32),
            jax.ShapeDtypeStruct(frame_wide.shape, F32),
        ],
        in_specs=[vmem] * 5,
        out_specs=[vmem] * 4,
        scratch_shapes=[
            pltpu.VMEM((3 * channels, (rows + 2) * cols), BF16),
            pltpu.VMEM((outs, rows * cols), F32),
            pltpu.VMEM((outs, rows * cols), BF16),
            pltpu.VMEM(frame_wide.shape, F32),
        ],
        compiler_params=pltpu.CompilerParams(vmem_limit_bytes=40 * 1024 * 1024),
    )(feature_flat, frame_wide, upstream, padded_weight, mirror_weight.T)


def both_ways(head, tail, axis):
    count = lax.axis_size(axis)
    ends = count - 1
    before = lax.ppermute(tail, axis, [(i, i + 1) for i in range(ends)])
    after = lax.ppermute(head, axis, [(i + 1, i) for i in range(ends)])
    return before, after


def shards(frames, features, cotangent, head_weight):
    taps = head_weight.shape[0] // 4
    padded_taps = -(-taps // 32) * 32
    rim = (taps - 1) // 2
    feature_map = features[0]
    channels, rows, cols = feature_map.shape
    image = frames[0]
    upstream = cotangent[0]
    lead = image.shape[:2]

    def packed(rim_rows, row):
        return jnp.concatenate([rim_rows.reshape(-1, cols), row.reshape(-1, cols)], 0)

    def unpacked(value):
        split = lead[0] * lead[1] * rim
        return value[:split].reshape(lead + (rim, cols)), value[split:].reshape(channels, 1, cols)

    before, after = both_ways(
        packed(image[:, :, :rim], feature_map[:, :1]),
        packed(image[:, :, rows - rim :], feature_map[:, rows - 1 :]),
        "tile",
    )
    image_before, row_before = unpacked(before)
    image_after, row_after = unpacked(after)
    extra = -(rows + 2 * rim) % 8
    extra += 0 if rows + 2 * rim + extra >= rows + padded_taps - 1 else 8
    frame_wide = jnp.concatenate(
        [image_before, image, image_after, jnp.zeros(lead + (extra, cols), BF16)], 2
    ).astype(F32)
    feature_flat = jnp.concatenate([row_before, feature_map, row_after], 1).reshape(
        channels, (rows + 2) * cols
    )
    by_group = head_weight.reshape(2, 2, taps, -1)

    def in_groups(vertical, horizontal, front):
        gap = padded_taps - taps
        return jnp.concatenate(
            [
                jnp.pad(vertical[:, None], ((0, 0), (0, 0), (0, gap), (0, 0))),
                jnp.pad(horizontal[:, None], ((0, 0), (0, 0), (front, gap - front), (0, 0))),
            ],
            1,
        ).reshape(4 * padded_taps, -1)

    back_front = mirror_front(taps, cols)
    padded_weight = in_groups(by_group[:, 0], by_group[:, 1], forward_front(taps))
    mirror_weight = in_groups(by_group[:, 0], by_group[:, 1, ::-1], back_front)

    weight_parts, feat_mid, feat_rims, image_grad = local_grads(
        feature_flat, frame_wide, upstream, padded_weight, mirror_weight, taps
    )
    before, after = both_ways(
        packed(image_grad[:, :, :rim], feat_rims[0]),
        packed(image_grad[:, :, rows + rim : rows + 2 * rim], feat_rims[1]),
        "tile",
    )
    image_before, row_before = unpacked(before)
    image_after, row_after = unpacked(after)
    middle = image_grad[:, :, rim : rim + rows]
    middle = middle.at[:, :, :rim].add(image_before).at[:, :, rows - rim :].add(image_after)
    feat_grad = jnp.concatenate(
        [feat_mid[:, :1] + row_before, feat_mid[:, 1 : rows - 1], feat_mid[:, rows - 1 :] + row_after], 1
    )

    weight_part = weight_parts
    for axis in ("dp", "tile"):
        count = lax.axis_size(axis)
        step = 1
        while step < count:
            weight_part = weight_part + lax.ppermute(
                weight_part, axis, [(i, i ^ step) for i in range(count)]
            )
            step *= 2
    weight_sum = weight_part.transpose(1, 0, 2).reshape(2, 2, padded_taps, -1)
    weight_sum = jnp.concatenate(
        [
            weight_sum[:, :1, :taps],
            weight_sum[:, 1:, back_front : back_front + taps][:, :, ::-1],
        ],
        1,
    ).reshape(4 * taps, -1)
    pixel_count = lax.axis_size("dp") * lax.axis_size("tile") * rows * cols
    return (weight_sum * pixel_count ** (-0.5), feat_grad[None], middle[None])


def solution(mesh):
    in_specs = (
        P("dp", None, None, "tile", None),
        P("dp", None, "tile", None),
        P("dp", None, "tile", None),
        P(),
    )
    out_specs = (P(), P("dp", None, "tile", None), P("dp", None, None, "tile", None))
    return jax.shard_map(shards, mesh=mesh, in_specs=in_specs, out_specs=out_specs, check_vma=False)
```

```python
import functools

import jax
import jax.numpy as jnp
from jax import lax
from jax.experimental import pallas as pl
from jax.experimental.pallas import tpu as pltpu
from jax.sharding import PartitionSpec as P

F32 = jnp.float32
BF16 = jnp.bfloat16
NN = (((1,), (0,)), ((), ()))
NT = (((1,), (1,)), ((), ()))
TN = (((0,), (0,)), ((), ()))


def mm(lhs, rhs, dims):
    return lax.dot_general(lhs, rhs, dims, preferred_element_type=F32)


def halves(value):
    high = value.astype(BF16)
    return high, (value - high.astype(F32)).astype(BF16)


def forward_front(tap_count):
    return -((tap_count - 1) // 2) % 8


def mirror_front(tap_count, cols):
    return (cols - 1 - (tap_count - 1) // 2) % 8


def natural_order(tap_count, padded_taps, cols):
    size = 4 * padded_taps
    out_at = lax.broadcasted_iota(jnp.int32, (size, size), 0)
    in_at = lax.broadcasted_iota(jnp.int32, (size, size), 1)
    chosen = jnp.full((size, size), -1, jnp.int32)
    for group in range(4):
        tap = out_at - group * tap_count
        place = tap if group % 2 == 0 else mirror_front(tap_count, cols) + tap_count - 1 - tap
        chosen = jnp.where((tap >= 0) & (tap < tap_count), group * padded_taps + place, chosen)
    return jnp.where(chosen == in_at, 1.0, 0.0).astype(BF16)


def skew(value, shift):
    count, cols = value.shape
    return jnp.concatenate(
        [
            pltpu.roll(value[row : row + 8], (shift + row) % cols, 1, stride=1, stride_axis=0)
            for row in range(0, count, 8)
        ],
        0,
    )


def local_kernel(
    tap_count,
    feat_ref,
    frame_ref,
    g_ref,
    w_ref,
    wt_ref,
    weight_ref,
    fgrad_ref,
    rims_ref,
    image_ref,
    patch_s,
    kern_s,
    kgrad_s,
    mirror_s,
    image_s,
):
    _, rows, cols = g_ref.shape
    channels = feat_ref.shape[0]
    padded_taps = w_ref.shape[0] // 4
    depth = 3 * channels
    rim = (tap_count - 1) // 2
    scale = tap_count ** (-0.5)
    lane = lax.broadcasted_iota(jnp.int32, (channels, cols), 1)
    first, last = lane == 0, lane == cols - 1

    for row in range(rows + 2):
        at = pl.ds(row * cols, cols)
        piece = feat_ref[:, at]
        wide = piece.astype(F32)
        patch_s[0:channels, at] = jnp.where(first, 0.0, pltpu.roll(wide, 1, 1)).astype(BF16)
        patch_s[channels : 2 * channels, at] = piece
        patch_s[2 * channels : depth, at] = jnp.where(
            last, 0.0, pltpu.roll(wide, cols - 1, 1)
        ).astype(BF16)

    group = 2
    for start in range(0, rows, group):
        stack = jnp.concatenate(
            [patch_s[:, (start + a) * cols : (start + a + group) * cols] for a in range(3)], 0
        )
        kern_s[:, start * cols : (start + group) * cols] = mm(w_ref[...], stack, NN) * scale

    image_s[...] = jnp.zeros_like(image_s)
    x_at = lax.broadcasted_iota(jnp.int32, (cols, cols), 0)
    q_at = lax.broadcasted_iota(jnp.int32, (cols, cols), 1)
    band = jnp.abs(q_at - x_at) <= rim
    natural = natural_order(tap_count, padded_taps, cols)
    mirror_band = jnp.abs(cols - 1 - q_at - x_at) <= rim
    in_second = q_at >= 2 * padded_taps
    front = forward_front(tap_count)
    back_shift = mirror_front(tap_count, cols) - (cols + rim - tap_count)

    mirror = jnp.where(q_at + x_at == cols - 1, 1.0, 0.0).astype(BF16)
    for f in range(2):
        for c in range(3):
            mirror_s[f, c] = mm(frame_ref[f, c].astype(BF16), mirror, NN)

    for y in range(rows):
        at = pl.ds(y * cols, cols)
        kern = kern_s[:, at]
        kern_t = jnp.transpose(kern)
        g_rows = [g_ref[c, y : y + 1, :] for c in range(3)]
        vert_parts, horiz_parts = [], []
        for f in range(2):
            base = (2 * f + 1) * padded_taps
            skewed = jnp.where(band, skew(kern_t, -(base + front + rim)), 0.0)
            k_high, k_low = halves(skewed)
            window, mirrored = [
                jnp.concatenate(
                    [ref[f, c, y : y + padded_taps, :] for c in range(3)], 0
                ).astype(BF16)
                for ref in (frame_ref, mirror_s)
            ]
            blend = mm(
                jnp.concatenate([window, window], 1), jnp.concatenate([k_high, k_low], 1), NT
            )
            grad_vert = g_rows[0] * blend[0:padded_taps]
            for c in range(1, 3):
                grad_vert += g_rows[c] * blend[c * padded_taps : (c + 1) * padded_taps]
            vert_parts.append(grad_vert)
            vertical = kern[2 * f * padded_taps : (2 * f + 1) * padded_taps]
            vg_high, vg_low = halves(jnp.concatenate([vertical * g for g in g_rows], 0))
            back = mm(
                jnp.concatenate([vg_high, vg_high], 1), jnp.concatenate([k_high, k_low], 0), NN
            )
            for c in range(3):
                image_s[f, c, y : y + padded_taps, :] += back[
                    c * padded_taps : (c + 1) * padded_taps
                ]
            cross = mm(
                jnp.concatenate([vg_high, vg_low], 0), jnp.concatenate([mirrored, mirrored], 0), TN
            )
            horiz_parts.append(skew(jnp.where(mirror_band, cross, 0.0), base + back_shift))
        horiz = jnp.transpose(jnp.where(in_second, horiz_parts[1], horiz_parts[0]))
        stacked = jnp.concatenate(
            [
                vert_parts[0],
                horiz[padded_taps : 2 * padded_taps],
                vert_parts[1],
                horiz[3 * padded_taps : 4 * padded_taps],
            ],
            0,
        )
        kgrad_s[:, at] = mm(natural, (stacked * scale).astype(BF16), NN).astype(BF16)

    for a in range(3):
        weight_ref[a * depth : (a + 1) * depth, :] = mm(
            patch_s[:, a * cols : (a + rows) * cols], kgrad_s[...], NT
        )

    for row in range(rows + 2):
        total = None
        for a in range(3):
            y = row - a
            if 0 <= y < rows:
                term = mm(
                    wt_ref[a * depth : (a + 1) * depth, :], kgrad_s[:, y * cols : (y + 1) * cols], NN
                )
                total = term if total is None else total + term
        left = total[0:channels]
        right = total[2 * channels : depth]
        result = (
            jnp.where(last, 0.0, pltpu.roll(left, cols - 1, 1))
            + total[channels : 2 * channels]
            + jnp.where(first, 0.0, pltpu.roll(right, 1, 1))
        )
        if row == 0:
            rims_ref[0, 0:channels] = result
        elif row == rows + 1:
            rims_ref[1, 0:channels] = result
        else:
            fgrad_ref[:, row - 1, :] = result

    for f in range(2):
        for c in range(3):
            start = channels + (3 * f + c) * rim
            rims_ref[0, start : start + rim] = image_s[f, c, 0:rim]
            rims_ref[1, start : start + rim] = image_s[f, c, rows + rim : rows + 2 * rim]
            image_ref[f, c] = image_s[f, c, rim : rows + rim]
    spare = channels + 6 * rim
    if spare < rims_ref.shape[1]:
        rims_ref[:, spare:] = jnp.zeros((2, rims_ref.shape[1] - spare, cols), F32)


def local_grads(feature_flat, frame_wide, upstream, padded_weight, flipped_weight, tap_count, rim_size):
    _, rows, cols = upstream.shape
    channels = feature_flat.shape[0]
    outs = padded_weight.shape[0]
    vmem = pl.BlockSpec(memory_space=pltpu.VMEM)
    return pl.pallas_call(
        functools.partial(local_kernel, tap_count),
        out_shape=[
            jax.ShapeDtypeStruct((9 * channels, outs), F32),
            jax.ShapeDtypeStruct((channels, rows, cols), F32),
            jax.ShapeDtypeStruct((2, rim_size, cols), F32),
            jax.ShapeDtypeStruct((2, 3, rows, cols), F32),
        ],
        in_specs=[vmem] * 5,
        out_specs=[vmem] * 4,
        scratch_shapes=[
            pltpu.VMEM((3 * channels, (rows + 2) * cols), BF16),
            pltpu.VMEM((outs, rows * cols), F32),
            pltpu.VMEM((outs, rows * cols), BF16),
            pltpu.VMEM(frame_wide.shape, F32),
            pltpu.VMEM(frame_wide.shape, F32),
        ],
        compiler_params=pltpu.CompilerParams(vmem_limit_bytes=40 * 1024 * 1024),
    )(feature_flat, frame_wide, upstream, padded_weight, flipped_weight)


def greet(peers):
    barrier = pltpu.get_barrier_semaphore()
    for peer in peers:
        pl.semaphore_signal(barrier, inc=1, device_id=peer, device_id_type=pl.DeviceIdType.MESH)
    pl.semaphore_wait(barrier, len(peers))


def push(source, target, send_sem, recv_sem, peer):
    return pltpu.make_async_remote_copy(
        src_ref=source,
        dst_ref=target,
        send_sem=send_sem,
        recv_sem=recv_sem,
        device_id=peer,
        device_id_type=pl.DeviceIdType.MESH,
    )


class Neighbours:
    def __init__(self, count, rims_ref, landed, send_sems, recv_sems):
        dp, tile = lax.axis_index("dp"), lax.axis_index("tile")
        self.has = (tile > 0, tile < count - 1)
        peers = ((dp, lax.max(tile - 1, 0)), (dp, lax.min(tile + 1, count - 1)))
        self.peers, self.landed = peers, landed
        self.out = [
            push(rims_ref.at[side], landed.at[1 - side], send_sems.at[side], recv_sems.at[1 - side], peers[side])
            for side in range(2)
        ]
        self.into = [
            push(rims_ref.at[side], landed.at[side], send_sems.at[side], recv_sems.at[side], peers[side])
            for side in range(2)
        ]

    def start(self):
        for side in range(2):
            pl.when(self.has[side])(self.out[side].start)

    def finish(self, out_ref):
        for side in range(2):

            @pl.when(self.has[side])
            def _():
                self.into[side].wait_recv()
                out_ref[side] = self.landed[side]
                self.out[side].wait_send()

            @pl.when(jnp.logical_not(self.has[side]))
            def _():
                out_ref[side] = jnp.zeros(out_ref.shape[1:], out_ref.dtype)


def halo_kernel(count, rims_ref, out_ref, landed, send_sems, recv_sems):
    near = Neighbours(count, rims_ref, landed, send_sems, recv_sems)
    barrier = pltpu.get_barrier_semaphore()
    for side in range(2):

        @pl.when(near.has[side])
        def _():
            pl.semaphore_signal(
                barrier, inc=1, device_id=near.peers[side], device_id_type=pl.DeviceIdType.MESH
            )

    pl.semaphore_wait(barrier, sum(has.astype(jnp.int32) for has in near.has))
    near.start()
    near.finish(out_ref)


def exchange_halo(rims):
    vmem = pl.BlockSpec(memory_space=pltpu.VMEM)
    return pl.pallas_call(
        functools.partial(halo_kernel, lax.axis_size("tile")),
        out_shape=jax.ShapeDtypeStruct(rims.shape, rims.dtype),
        in_specs=[vmem],
        out_specs=vmem,
        scratch_shapes=[
            pltpu.VMEM(rims.shape, rims.dtype),
            pltpu.SemaphoreType.DMA((2,)),
            pltpu.SemaphoreType.DMA((2,)),
        ],
        compiler_params=pltpu.CompilerParams(collective_id=0, has_side_effects=True),
    )(rims)


def plan(dp_count, tile_count):
    low = 1
    while tile_count * low * 2 <= 8 and dp_count % (low * 2) == 0:
        low *= 2
    left, radices = dp_count // low, []
    while left > 1:
        radix = 4 if left % 4 == 0 else 2 if left % 2 == 0 else left
        radices.append(radix)
        left //= radix
    return low, radices


def total_kernel(
    tile_count, low, radices, factor, weight_ref, rims_ref, sum_ref, rims_out_ref,
    landed, first_s, stage_s, gather_s, rim_sems, first_sems, stage_sems, gather_sems,
):
    dp, tile = lax.axis_index("dp"), lax.axis_index("tile")
    size = low * tile_count
    share = weight_ref.shape[0] // size
    own = lax.rem(dp, low) * tile_count + tile
    inner = []
    for step in range(1, size):
        place = lax.rem(own + step, size)
        inner.append((place, (dp - lax.rem(dp, low) + place // tile_count, lax.rem(place, tile_count))))
    outer, unit = [], low
    for radix in radices:
        digit = lax.rem(dp // unit, radix)
        peers = [
            (dp + (lax.rem(digit + step, radix) - digit) * unit, tile) for step in range(1, radix)
        ]
        outer.append((digit, peers))
        unit *= radix
    near = Neighbours(tile_count, rims_ref, landed, rim_sems.at[0], rim_sems.at[1])

    greet([peer for _, peer in inner] + [peer for _, peers in outer for peer in peers])
    copies = []
    first = []
    for step, (place, peer) in enumerate(inner):
        start = pl.multiple_of(place * share, 8)
        first.append(
            push(weight_ref.at[pl.ds(start, share)], first_s.at[step], first_sems.at[0, step], first_sems.at[1, step], peer)
        )
        first[-1].start()
    near.start()
    total = weight_ref[pl.ds(pl.multiple_of(own * share, 8), share), :]
    for step in range(size - 1):
        first[step].wait_recv()
        total = total + first_s[step]
    copies += first

    for stage, (digit, peers) in enumerate(outer):
        stage_s[stage, digit] = total
        moves = []
        for step, peer in enumerate(peers):
            slot = stage_s.at[stage, digit]
            moves.append(push(slot, slot, stage_sems.at[0, stage, step], stage_sems.at[1, stage, step], peer))
            moves[-1].start()
        for move in moves:
            move.wait_recv()
        total = stage_s[stage, 0]
        for place in range(1, radices[stage]):
            total = total + stage_s[stage, place]
        copies += moves

    gather_s[own] = total * factor
    moves = []
    for step, (_, peer) in enumerate(inner):
        slot = gather_s.at[own]
        moves.append(push(slot, slot, gather_sems.at[0, step], gather_sems.at[1, step], peer))
        moves[-1].start()
    near.finish(rims_out_ref)
    for move in moves:
        move.wait_recv()
    for place in range(size):
        sum_ref[place * share : (place + 1) * share, :] = gather_s[place]
    for copy in copies + moves:
        copy.wait_send()


def total_weight(weight_part, rims, pixel_count):
    dp_count, tile_count = lax.axis_size("dp"), lax.axis_size("tile")
    low, radices = plan(dp_count, tile_count)
    size = low * tile_count
    rows, cols = weight_part.shape
    widest = max(radices + [2])
    stages = max(len(radices), 1)
    share = -(-rows // (8 * size)) * 8
    weight_part = jnp.pad(weight_part, ((0, share * size - rows), (0, 0)))
    vmem = pl.BlockSpec(memory_space=pltpu.VMEM)
    others = max(size - 1, 1)
    dma = pltpu.SemaphoreType.DMA
    total, rims = pl.pallas_call(
        functools.partial(total_kernel, tile_count, low, tuple(radices), pixel_count ** (-0.5)),
        out_shape=[
            jax.ShapeDtypeStruct(weight_part.shape, F32),
            jax.ShapeDtypeStruct(rims.shape, F32),
        ],
        in_specs=[vmem] * 2,
        out_specs=[vmem] * 2,
        scratch_shapes=[
            pltpu.VMEM(rims.shape, F32),
            pltpu.VMEM((others, share, cols), F32),
            pltpu.VMEM((stages, widest, share, cols), F32),
            pltpu.VMEM((size, share, cols), F32),
            dma((2, 2)),
            dma((2, others)),
            dma((2, stages, widest - 1)),
            dma((2, others)),
        ],
        compiler_params=pltpu.CompilerParams(
            collective_id=1, has_side_effects=True, vmem_limit_bytes=40 * 1024 * 1024
        ),
    )(weight_part, rims)
    return total[:rows], rims


def shards(frames, features, cotangent, head_weight):
    taps = head_weight.shape[0] // 4
    padded_taps = -(-taps // 32) * 32
    rim = (taps - 1) // 2
    feature_map = features[0]
    channels, rows, cols = feature_map.shape
    image = frames[0]
    upstream = cotangent[0]
    lead = image.shape[:2]

    rim_size = -(-(channels + lead[0] * lead[1] * rim) // 16) * 16

    def packed(rim_rows, row):
        both = jnp.concatenate([row.reshape(-1, cols), rim_rows.reshape(-1, cols)], 0)
        return jnp.pad(both, ((0, rim_size - both.shape[0]), (0, 0)))

    def unpacked(value):
        used = channels + lead[0] * lead[1] * rim
        return value[channels:used].reshape(lead + (rim, cols)), value[:channels].reshape(channels, 1, cols)

    halo = exchange_halo(
        jnp.stack(
            [
                packed(image[:, :, :rim], feature_map[:, :1]),
                packed(image[:, :, rows - rim :], feature_map[:, rows - 1 :]),
            ]
        )
    )
    image_before, row_before = unpacked(halo[0])
    image_after, row_after = unpacked(halo[1])
    extra = -(rows + 2 * rim) % 8
    extra += 0 if rows + 2 * rim + extra >= rows + padded_taps - 1 else 8
    frame_wide = jnp.concatenate(
        [image_before, image, image_after, jnp.zeros(lead + (extra, cols), BF16)], 2
    ).astype(F32)
    feature_flat = jnp.concatenate([row_before, feature_map, row_after], 1).reshape(
        channels, (rows + 2) * cols
    )
    by_group = head_weight.reshape(2, 2, taps, -1)
    gap = padded_taps - taps
    front = forward_front(taps)
    padded_weight = jnp.concatenate(
        [
            jnp.pad(by_group[:, :1], ((0, 0), (0, 0), (0, gap), (0, 0))),
            jnp.pad(by_group[:, 1:], ((0, 0), (0, 0), (front, gap - front), (0, 0))),
        ],
        1,
    ).reshape(4 * padded_taps, -1)
    flipped_weight = jnp.pad(head_weight, ((0, 4 * gap), (0, 0))).T

    weight_part, feat_mid, rims, middle = local_grads(
        feature_flat, frame_wide, upstream, padded_weight, flipped_weight, taps, rim_size
    )
    pixel_count = lax.axis_size("dp") * lax.axis_size("tile") * rows * cols
    weight_sum, halo = total_weight(weight_part, rims, pixel_count)
    image_before, row_before = unpacked(halo[0])
    image_after, row_after = unpacked(halo[1])
    middle = middle.at[:, :, :rim].add(image_before).at[:, :, rows - rim :].add(image_after)
    feat_grad = feat_mid.at[:, :1].add(row_before).at[:, rows - 1 :].add(row_after)
    return (weight_sum[:, : 4 * taps].T, feat_grad[None], middle[None])


def solution(mesh):
    in_specs = (
        P("dp", None, None, "tile", None),
        P("dp", None, "tile", None),
        P("dp", None, "tile", None),
        P(),
    )
    out_specs = (P(), P("dp", None, "tile", None), P("dp", None, None, "tile", None))
    return jax.shard_map(shards, mesh=mesh, in_specs=in_specs, out_specs=out_specs, check_vma=False)
```
